512 devices in a mesh: prow: 16 (over z_hi, y, core), pcol: 32 (over x, z_lo).
Axes of the slice: x: 4, y: 4, z: 16 (z_hi: 2, z_lo: 8; z = z_hi * 8 + z_lo), core: 2. Of those that a mesh axis runs over, the one named last changes fastest.
Arguments:
- ainv: bfloat16 [16384, 16384], P('pcol', 'prow'), may hold values from -6 to 6
- lpanel: bfloat16 [16384, 2048], P('prow', 'pcol'), may hold values from -0.0625 to 0.0625
- dinv: float32 [256, 2048], P(None, 'prow'), may hold values from -6 to 6
- rowblocks: int32 [8, 40], replicated, may hold values from 0 to 63, as said below
- counts: int32 [8], replicated, may hold values from 30 to 40
- widths: int32 [8], replicated, may hold values from 1 to 256, 1536 in all
Outputs:
- selected_inverse: bfloat16 [16384, 2048], P('pcol', 'prow')
- diagonal_blocks: float32 [256, 2048], P(None, 'prow')
The draws below stay inside these ranges and needn't reach their ends.
Inputs may be any that keep to these rules, and one draw needn't show every extreme that they name: The entries of one row of rowblocks are distinct; only the first counts[k] entries of row k belong to supernode k. The widths sum to 1536.
All inputs are finite; a program needn't handle non-finite values.
Results may differ from the reference program's by a relative error of at most 0.02.
Values may be sent and summed in bfloat16 or wider, within the bound.
No kernel may reach another device: no remote copies, remote signals or barrier semaphores. Data moves between devices by JAX's collectives and lax.ppermute only.
A program may use at most 64 MiB of HBM per device.

```python
import math
import jax
import jax.numpy as jnp
import numpy as np
from jax import lax

B = 256
SNODES = 8
NB = 64
RB = 4
SMAX = 40
N_PROW = 16


def draw_rowblocks(key, part):
    key = jax.random.fold_in(key, 11)
    node_keys = jax.random.split(key, SNODES)
    orders = jax.vmap(lambda single: jax.random.permutation(single, NB))(node_keys)
    return orders[:, :SMAX].astype(jnp.int32)


def draw_counts(key, part):
    key = jax.random.fold_in(key, 23)
    count_key, slot_key, other_key = jax.random.split(key, 3)
    fewest = 3 * SMAX // 4
    values = jax.random.randint(count_key, (SNODES,), fewest, SMAX + 1)
    target_slot = jax.random.randint(slot_key, (), 0, SNODES)
    other_slot = (target_slot + 1 + jax.random.randint(other_key, (), 0, SNODES - 1)) % SNODES
    values = values.at[target_slot].set(SMAX)
    values = values.at[other_slot].set(fewest)
    return values.astype(jnp.int32)


def steps_of(own_key, shape, pieces, smallest, largest):
    def one(position, parts):
        heights = jax.random.uniform(jax.random.fold_in(jax.random.fold_in(own_key, 6), position), (parts,), jnp.float32, smallest / len(pieces), largest / len(pieces))
        return jnp.repeat(jnp.exp(heights), shape[position] // parts).reshape((-1,) + (1,) * (len(shape) - position - 1))

    factor_of = one(*pieces[0])
    for cut in pieces[1:]:
        factor_of = factor_of * one(*cut)
    return factor_of


def profile(amount, total, most, slope):
    portions = [(1 << 20) // math.isqrt(grade ** slope) + 1 for grade in range(2, amount + 1)]
    rest, holding = total - most - (amount - 1), [1] * (amount - 1)
    while rest > 0:
        candidates = [i for i in range(amount - 1) if holding[i] < most]
        whole, remaining = sum([portions[i] for i in candidates]), rest
        for i in candidates:
            extra = min(most - holding[i], max(1, remaining * portions[i] // whole), rest)
            holding[i] = holding[i] + extra
            rest = rest - extra
    return np.array([most] + holding)


def ragged_sizes(own_key, number_of, total, reach, slope):
    if number_of == 2:
        one = jax.random.randint(own_key, (), max(1, total - reach), min(reach, total - 1) + 1)
        return jnp.stack([one, total - one])
    sizes = jnp.asarray(profile(number_of, total, reach, slope), jnp.int32)
    pairs = (number_of - 1) // 2
    donor, taker = sizes[1:1 + 2 * pairs:2], sizes[2:2 + 2 * pairs:2]
    margin = jnp.minimum(donor - 1, reach - taker)
    moved = jax.random.randint(jax.random.fold_in(own_key, 1), (pairs,), 0, 1 << 20) % (margin + 1)
    sizes = sizes.at[1:1 + 2 * pairs:2].set(donor - moved).at[2:2 + 2 * pairs:2].set(taker + moved)
    return sizes[jax.random.permutation(jax.random.fold_in(own_key, 2), number_of)]


def normal_values(key, extent, spread, reach, pieces=(), held_as=jnp.bfloat16):
    level = steps_of(key, extent, pieces, -0.22, 0.18) if pieces else 1.0
    array = jax.random.normal(key, extent, jnp.float32) * spread * level
    return jnp.minimum(jnp.maximum(array, -reach), reach).astype(held_as)


def setup_inputs(seed: int = 0) -> dict:
    keys = jax.random.split(jax.random.key(seed), 7)
    ainv = normal_values(keys[0], (NB * B, NB * B), 1.0, 6.0, ((0, 32), (1, 16)))
    lpanel = normal_values(keys[1], (NB * B, SNODES * B), (SMAX * B) ** -0.5, 0.0625, ((0, 16), (1, 32)))
    dinv = normal_values(keys[2], (B, SNODES * B), 1.0, 6.0, ((1, 16),), jnp.float32)
    rowblocks = draw_rowblocks(jax.random.fold_in(keys[6], 71), 0)
    counts = draw_counts(jax.random.fold_in(keys[6], 71), 0)
    widths = ragged_sizes(keys[5], SNODES, SNODES * B * 3 // 4, B, 2).astype(jnp.int32)
    return dict(ainv=ainv, lpanel=lpanel, dinv=dinv, rowblocks=rowblocks, counts=counts, widths=widths)


def one_supernode(ainv, lpanel, dinv, rowblocks, counts, widths, supernode):
    struct_rows = rowblocks[supernode]
    slot_live = jnp.arange(SMAX, dtype=jnp.int32) < counts[supernode]
    column_live = jnp.arange(B, dtype=jnp.int32) < widths[supernode]
    row_index = (struct_rows[:, None] * B + jnp.arange(B, dtype=jnp.int32)[None, :]).reshape(SMAX * B).astype(jnp.int32)
    first_col = (supernode * B).astype(jnp.int32)
    panel_cols = lax.dynamic_slice_in_dim(lpanel, first_col, B, 1)
    factor = panel_cols[row_index].reshape(SMAX, B, B)
    keep_mask = slot_live[:, None, None] & column_live[None, None, :]
    factor = jnp.where(keep_mask, factor, jnp.zeros((), jnp.bfloat16))
    inverse_rows = ainv[row_index]
    inverse_sub = inverse_rows[:, row_index].reshape(SMAX * B, SMAX, B).astype(jnp.float32)
    factor_wide = factor.astype(jnp.float32)
    products = jnp.einsum("itb,tbc->tic", inverse_sub, factor_wide, precision=lax.Precision.HIGHEST)
    group_rows = struct_rows // RB
    member = ((group_rows[None, :] == jnp.arange(N_PROW, dtype=jnp.int32)[:, None]) & slot_live[None, :]).astype(jnp.float32)
    partials = jnp.einsum("gt,tic->gic", member, products, precision=lax.Precision.HIGHEST)
    rounded = lax.optimization_barrier(partials.astype(jnp.bfloat16)).astype(jnp.float32)
    selected = jnp.sum(rounded, axis=0)
    row_live = jnp.repeat(slot_live, B)[:, None]
    offdiag = jnp.where(row_live, -selected, jnp.zeros((), jnp.float32)).astype(jnp.bfloat16)
    quadratic = jnp.einsum("sbc,sbd->cd", factor_wide, selected.reshape(SMAX, B, B), precision=lax.Precision.HIGHEST)
    corner = column_live[:, None] & column_live[None, :]
    own_inverse = lax.dynamic_slice_in_dim(dinv, first_col, B, 1)
    diagonal = jnp.where(corner, own_inverse, jnp.zeros((), jnp.float32)) + quadratic
    return offdiag, row_index, diagonal


def reference(ainv, lpanel, dinv, rowblocks, counts, widths):
    def visit_node(supernode):
        return one_supernode(ainv, lpanel, dinv, rowblocks, counts, widths, supernode)

    offdiag_parts, row_parts, diagonal_parts = lax.map(visit_node, jnp.arange(SNODES, dtype=jnp.int32))
    column_index = (jnp.arange(SNODES, dtype=jnp.int32)[:, None] * B + jnp.arange(B, dtype=jnp.int32)[None, :]).astype(jnp.int32)
    selected_inverse = jnp.zeros((NB * B, SNODES * B), jnp.bfloat16)
    selected_inverse = selected_inverse.at[row_parts[:, :, None], column_index[:, None, :]].set(offdiag_parts)
    diagonal_blocks = jnp.transpose(diagonal_parts, (1, 0, 2)).reshape(B, SNODES * B)
    return selected_inverse, diagonal_blocks
```

```python
import jax
import jax.numpy as jnp
from jax import lax
from jax.sharding import PartitionSpec as P

B = 256
SNODES = 8
AXES = ("prow", "pcol")
CONTRACT_LAST = (((1,), (1,)), ((), ()))


def send(value, target):
    pairs = []
    for source in range(512):
        row, col = source // 32, source % 32
        zh, y, core, x, zl = target(row >> 3, (row >> 1) & 3, row & 1, col >> 3, col & 7)
        pairs.append((source, ((zh * 4 + y) * 2 + core) * 32 + x * 8 + zl))
    return lax.ppermute(value, AXES, pairs)


def fold_x(zh, y, core, x, zl, flip):
    node = 2 * x + (zl >> 2)
    return (zh, y, core, node & 3, (((node >> 2) ^ flip) << 2) | (zl & 3))


def rows_home(zh, y, core, x, zl):
    return (zl >> 2, x, (zl >> 1) & 1, (zh << 1) | (y >> 1), ((y & 1) << 2) | (core << 1) | (zl & 1))


def dot_t(left, right):
    return lax.dot_general(left, right, CONTRACT_LAST, preferred_element_type=jnp.float32)


def flip_if(value, bit, axis):
    return jnp.where(bit == 0, value, jnp.flip(value, axis))


def per_device(ainv, lpanel, dinv, rowblocks, counts, widths):
    prow, pcol = lax.axis_index("prow"), lax.axis_index("pcol")
    zh, y, core = prow >> 3, (prow >> 1) & 3, prow & 1
    x, zl = pcol >> 3, pcol & 7
    high, mid, low = zl >> 2, (zl >> 1) & 1, zl & 1

    own = lpanel.T
    first = send(own, lambda *d: fold_x(*d, 0))
    second = send(own, lambda *d: fold_x(*d, 1))
    pair = jnp.stack([first, second])
    near = send(pair, lambda zh, y, core, x, zl: (zh, y, core, x, zl ^ 2))
    quad = jnp.stack([pair, near], axis=1)
    last = send(quad, lambda zh, y, core, x, zl: (zh, y, core, x, zl ^ 1))

    a1 = send(ainv, lambda zh, y, core, x, zl: (zh, y, core, x ^ 1, zl))
    a3 = send(ainv, lambda zh, y, core, x, zl: (zh, y, core, x ^ 3, zl))
    half = ainv.shape[0] // 2
    a2 = [
        send(a3[:half], lambda zh, y, core, x, zl: (zh, y, core, x ^ 1, zl)),
        send(a1[half:], lambda zh, y, core, x, zl: (zh, y, core, x ^ 3, zl)),
    ]
    a2 = jnp.concatenate(a2, axis=0)

    slots = jnp.arange(rowblocks.shape[1], dtype=jnp.int32)
    used = jnp.where(slots[None, :] < counts[:, None], rowblocks, -1)
    member = jnp.any(used[:, :, None] == jnp.arange(64, dtype=jnp.int32)[None, None, :], axis=1)
    nodes = jnp.arange(SNODES, dtype=jnp.int32)
    my_nodes = (high ^ jnp.arange(2, dtype=jnp.int32)) * 4 + x
    chosen = my_nodes[:, None] == nodes[None, :]
    my_blocks = prow * 4 + jnp.arange(4, dtype=jnp.int32)
    block_is = my_blocks[:, None] == jnp.arange(64, dtype=jnp.int32)[None, :]
    live = jnp.any(
        chosen[:, None, :, None] & block_is[None, :, None, :] & member[None, None, :, :], axis=(2, 3)
    )
    width = jnp.sum(jnp.where(chosen, widths[None, :], 0), axis=1)
    quarter = (
        (mid ^ jnp.arange(2, dtype=jnp.int32))[:, None] * 2
        + (low ^ jnp.arange(2, dtype=jnp.int32))[None, :]
    )
    within = quarter[:, :, None] * 64 + jnp.arange(64, dtype=jnp.int32)[None, None, :]
    active = within[None] < width[:, None, None, None]

    factor = jnp.stack([quad, last], axis=2)
    keep_mask = active[..., None, None] & live[:, None, None, None, :, None]
    factor = jnp.where(
        keep_mask, factor.reshape(2, 2, 2, 64, 4, B), jnp.zeros((), jnp.bfloat16)
    ).reshape(2, 2, 2, 64, 1024)

    mine = lax.dynamic_slice_in_dim(factor[0], low * 512, 512, axis=3)
    across = send(mine, rows_home)

    keep = core ^ mid
    theirs = lax.dynamic_index_in_dim(factor, 1 - keep, 1, keepdims=False).reshape(256, 1024)
    ours = lax.dynamic_index_in_dim(factor, keep, 1, keepdims=False).reshape(256, 1024)
    blocks = [ainv, a1, a2, a3]
    away = jnp.stack([dot_t(theirs, block).astype(jnp.bfloat16) for block in blocks])
    other = send(away, lambda zh, y, core, x, zl: (zh, y, core ^ 1, x, zl))
    here = jnp.stack([dot_t(ours, block) for block in blocks])
    chip = (here + other.astype(jnp.float32)).astype(jnp.bfloat16)

    total = None
    for k in range(4):
        share = lax.dynamic_index_in_dim(chip, y ^ k ^ x, 0, keepdims=False)
        came = send(share, lambda zh, y, core, x, zl: (zh, x, core, y ^ k, zl)).astype(jnp.float32)
        total = came if total is None else total + came
    total = total.reshape(2, 128, 512)

    stay = zh ^ high
    leave = lax.dynamic_index_in_dim(total, 1 - stay, 0, keepdims=False).astype(jnp.bfloat16)
    came = send(leave, lambda zh, y, core, x, zl: (zh ^ 1, y, core, x, zl))
    product = lax.dynamic_index_in_dim(total, stay, 0, keepdims=False) + came.astype(jnp.float32)
    product = flip_if(product.reshape(2, 64, 512), low, 0).reshape(128, 512)

    node = prow >> 1
    row_ids = pcol * 2 + jnp.arange(2, dtype=jnp.int32)
    kept = jnp.any(
        (row_ids[:, None] == jnp.arange(64, dtype=jnp.int32)[None, :])[:, None, :]
        & (nodes == node)[None, :, None]
        & member[None],
        axis=(1, 2),
    )
    negated = jnp.where(kept[None, :, None], -product.reshape(128, 2, B), 0.0).reshape(128, 512)
    selected_inverse = negated.astype(jnp.bfloat16).T

    terms = dot_t(across.reshape(256, 512), product.astype(jnp.bfloat16))
    terms = flip_if(flip_if(terms.reshape(2, 2, 64, 128), low, 1), core, 0).reshape(256, 128)
    terms = terms.astype(jnp.bfloat16)
    by_x = [terms] + [
        send(terms, lambda zh, y, core, x, zl: (zh, y, core, x ^ k, zl)) for k in (1, 2, 3)
    ]
    by_x = [part.astype(jnp.float32) for part in by_x]
    terms = (by_x[0] + by_x[1]) + (by_x[2] + by_x[3])
    for bit in (4, 2, 1):
        sent = terms.astype(jnp.bfloat16)
        came = send(sent, lambda zh, y, core, x, zl: (zh, y, core, x, zl ^ bit))
        terms = sent.astype(jnp.float32) + came.astype(jnp.float32)

    my_width = jnp.sum(jnp.where(nodes == node, widths, 0))
    column = core * 128 + jnp.arange(128, dtype=jnp.int32)
    corner = (jnp.arange(B, dtype=jnp.int32)[:, None] < my_width) & (column < my_width)[None, :]
    diagonal_blocks = jnp.where(corner, dinv, 0.0) + terms
    return (selected_inverse, diagonal_blocks)


def solution(mesh):
    placed = (P("pcol", "prow"), P("prow", "pcol"), P(None, "prow"), P(), P(), P())
    return jax.shard_map(
        per_device,
        mesh=mesh,
        in_specs=placed,
        out_specs=(P("pcol", "prow"), P(None, "prow")),
        check_vma=False,
    )
```

```python
import jax
import jax.numpy as jnp
from jax import lax
from jax.sharding import PartitionSpec as P

B = 256
SNODES = 8
AXES = ("prow", "pcol")
CONTRACT_LAST = (((1,), (1,)), ((), ()))


def send(value, target):
    pairs = []
    for source in range(512):
        row, col = source // 32, source % 32
        zh, y, core, x, zl = target(row >> 3, (row >> 1) & 3, row & 1, col >> 3, col & 7)
        pairs.append((source, ((zh * 4 + y) * 2 + core) * 32 + x * 8 + zl))
    return lax.ppermute(value, AXES, pairs)


def fold_x(zh, y, core, x, zl, flip):
    node = 2 * x + (zl >> 2)
    return (zh, y, core, node & 3, (((node >> 2) ^ flip) << 2) | (zl & 3))


def rows_home(zh, y, core, x, zl):
    return (zl >> 2, x, (zl >> 1) & 1, (zh << 1) | (y >> 1), ((y & 1) << 2) | (core << 1) | (zl & 1))


def swap_groups():
    groups = []
    for zh in range(2):
        for core in range(2):
            for x in range(4):
                for zl in range(8):
                    groups.append(
                        [((zh * 4 + (j ^ x)) * 2 + core) * 32 + x * 8 + zl for j in range(4)]
                    )
    return groups


def dot_t(left, right):
    return lax.dot_general(left, right, CONTRACT_LAST, preferred_element_type=jnp.float32)


def per_device(ainv, lpanel, dinv, rowblocks, counts, widths):
    prow, pcol = lax.axis_index("prow"), lax.axis_index("pcol")
    zh, y, core = prow >> 3, (prow >> 1) & 3, prow & 1
    x, zl = pcol >> 3, pcol & 7
    high, mid, low = zl >> 2, (zl >> 1) & 1, zl & 1

    own = lpanel.T
    first = send(own, lambda *d: fold_x(*d, 0))
    second = send(own, lambda *d: fold_x(*d, 1))
    pair = jnp.stack([first, second])
    near = send(pair, lambda zh, y, core, x, zl: (zh, y, core, x, zl ^ 2))
    quad = jnp.stack([pair, near], axis=1)
    last = send(quad, lambda zh, y, core, x, zl: (zh, y, core, x, zl ^ 1))

    a1 = send(ainv, lambda zh, y, core, x, zl: (zh, y, core, x ^ 1, zl))
    a3 = send(ainv, lambda zh, y, core, x, zl: (zh, y, core, x ^ 3, zl))
    half = ainv.shape[0] // 2
    a2 = [
        send(a3[:half], lambda zh, y, core, x, zl: (zh, y, core, x ^ 1, zl)),
        send(a1[half:], lambda zh, y, core, x, zl: (zh, y, core, x ^ 3, zl)),
    ]
    last, upper, lower = lax.optimization_barrier((last, *a2))
    a2 = jnp.concatenate([upper, lower], axis=0)

    slots = jnp.arange(rowblocks.shape[1], dtype=jnp.int32)
    used = jnp.where(slots[None, :] < counts[:, None], rowblocks, -1)
    member = jnp.any(used[:, :, None] == jnp.arange(64, dtype=jnp.int32)[None, None, :], axis=1)
    nodes = jnp.arange(SNODES, dtype=jnp.int32)
    my_nodes = (high ^ jnp.arange(2, dtype=jnp.int32)) * 4 + x
    chosen = my_nodes[:, None] == nodes[None, :]
    my_blocks = prow * 4 + jnp.arange(4, dtype=jnp.int32)
    block_is = my_blocks[:, None] == jnp.arange(64, dtype=jnp.int32)[None, :]
    live = jnp.any(
        chosen[:, None, :, None] & block_is[None, :, None, :] & member[None, None, :, :], axis=(2, 3)
    )
    width = jnp.sum(jnp.where(chosen, widths[None, :], 0), axis=1)
    half_of = (mid ^ jnp.arange(2, dtype=jnp.int32))[:, None, None] * 128
    within = half_of + jnp.arange(128, dtype=jnp.int32).reshape(1, 2, 64)
    active = within[None] < width[:, None, None, None]

    factor = jnp.stack(
        [jnp.where(low == 0, quad, last), jnp.where(low == 0, last, quad)], axis=2
    )
    row_scale = jnp.repeat(live.astype(jnp.bfloat16), B, axis=1)
    factor = factor * active[..., None].astype(jnp.bfloat16) * row_scale[:, None, None, None, :]

    mine = lax.dynamic_slice_in_dim(factor[0, 0].reshape(128, 1024), low * 512, 512, axis=1)
    mine = send(mine, rows_home)

    keep = core ^ mid
    theirs = lax.dynamic_index_in_dim(factor, 1 - keep, 1, keepdims=False).reshape(256, 1024)
    ours = lax.dynamic_index_in_dim(factor, keep, 1, keepdims=False).reshape(256, 1024)
    blocks = [ainv, a1, a2, a3]
    away = jnp.stack([dot_t(theirs, block).astype(jnp.bfloat16) for block in blocks])
    other = send(away, lambda zh, y, core, x, zl: (zh, y, core ^ 1, x, zl))
    here = jnp.stack([dot_t(ours, block) for block in blocks])
    chip = (here + other.astype(jnp.float32)).astype(jnp.bfloat16)

    chip, mine = lax.optimization_barrier((chip, mine))
    shares = lax.all_to_all(chip, AXES, 0, 0, axis_index_groups=swap_groups())
    beside = send(mine, lambda zh, y, core, x, zl: (zh, y, core ^ 1, x, zl))
    across = jnp.concatenate([jnp.where(core == 0, mine, beside), jnp.where(core == 0, beside, mine)])
    rounded = jnp.sum(shares.astype(jnp.float32), axis=0).reshape(2, 128, 512).astype(jnp.bfloat16)

    stay = zh ^ high
    part = [lax.dynamic_index_in_dim(rounded, stay ^ k, 0, keepdims=False) for k in range(2)]
    far = send(part[1], lambda zh, y, core, x, zl: (zh ^ 1, x, core, y, zl))
    near = send(part[0], lambda zh, y, core, x, zl: (zh, x, core, y, zl))
    product = near.astype(jnp.float32) + far.astype(jnp.float32)

    terms = dot_t(across, product.astype(jnp.bfloat16)).astype(jnp.bfloat16)
    pieces = lax.all_to_all(terms.reshape(32, 8, 128), "pcol", 0, 0)
    piece = jnp.sum(pieces.astype(jnp.float32), axis=0).astype(jnp.bfloat16)
    terms = lax.all_to_all(jnp.broadcast_to(piece[None], (32, 8, 128)), "pcol", 0, 0)
    terms = terms.reshape(256, 128).astype(jnp.float32)

    node = prow >> 1
    row_ids = pcol * 2 + jnp.arange(2, dtype=jnp.int32)
    kept = jnp.any(
        (row_ids[:, None] == jnp.arange(64, dtype=jnp.int32)[None, :])[:, None, :]
        & (nodes == node)[None, :, None]
        & member[None],
        axis=(1, 2),
    )
    negated = jnp.where(kept[None, :, None], -product.reshape(128, 2, B), 0.0).reshape(128, 512)
    selected_inverse = negated.astype(jnp.bfloat16).T

    my_width = jnp.sum(jnp.where(nodes == node, widths, 0))
    column = core * 128 + jnp.arange(128, dtype=jnp.int32)
    corner = (jnp.arange(B, dtype=jnp.int32)[:, None] < my_width) & (column < my_width)[None, :]
    diagonal_blocks = jnp.where(corner, dinv, 0.0) + terms
    return (selected_inverse, diagonal_blocks)


def solution(mesh):
    placed = (P("pcol", "prow"), P("prow", "pcol"), P(None, "prow"), P(), P(), P())
    return jax.shard_map(
        per_device,
        mesh=mesh,
        in_specs=placed,
        out_specs=(P("pcol", "prow"), P(None, "prow")),
        check_vma=False,
    )
```

```python
import functools

import jax
import jax.numpy as jnp
from jax import lax
from jax.experimental import pallas as pl
from jax.experimental.pallas import tpu as pltpu
from jax.sharding import PartitionSpec as P

B = 256
SNODES = 8
AXES = ("prow", "pcol")
CONTRACT_LAST = (((1,), (1,)), ((), ()))


def send(value, target):
    pairs = []
    for source in range(512):
        row, col = source // 32, source % 32
        zh, y, core, x, zl = target(row >> 3, (row >> 1) & 3, row & 1, col >> 3, col & 7)
        pairs.append((source, ((zh * 4 + y) * 2 + core) * 32 + x * 8 + zl))
    return lax.ppermute(value, AXES, pairs)


def fold_x(zh, y, core, x, zl, flip):
    node = 2 * x + (zl >> 2)
    return (zh, y, core, node & 3, (((node >> 2) ^ flip) << 2) | (zl & 3))


def rows_home(zh, y, core, x, zl):
    return (zl >> 2, x, (zl >> 1) & 1, (zh << 1) | (y >> 1), ((y & 1) << 2) | (core << 1) | (zl & 1))


def swap_groups():
    groups = []
    for zh in range(2):
        for core in range(2):
            for x in range(4):
                for zl in range(8):
                    groups.append(
                        [((zh * 4 + (j ^ x)) * 2 + core) * 32 + x * 8 + zl for j in range(4)]
                    )
    return groups


def dot_t(left, right):
    return lax.dot_general(left, right, CONTRACT_LAST, preferred_element_type=jnp.float32)


def product_kernel(added, factor, near, one, upper, lower, three, *rest):
    out = rest[-1]
    half = upper.shape[0]
    for place, rows in ((0, near), (1, one), (3, three)):
        term = dot_t(factor[...], rows[...])
        if added:
            term = term + rest[0][place].astype(jnp.float32)
        out[place] = term.astype(jnp.bfloat16)
    for columns, rows in ((slice(0, half), upper), (slice(half, 2 * half), lower)):
        term = dot_t(factor[...], rows[...])
        if added:
            term = term + rest[0][2, :, columns].astype(jnp.float32)
        out[2, :, columns] = term.astype(jnp.bfloat16)


def partial_product(factor, blocks, *added):
    width, depth = factor.shape
    height = blocks[0].shape[0]
    return pl.pallas_call(
        functools.partial(product_kernel, len(added)),
        in_specs=[pl.BlockSpec(memory_space=pltpu.VMEM)] * (6 + len(added)),
        out_specs=pl.BlockSpec(memory_space=pltpu.VMEM),
        out_shape=jax.ShapeDtypeStruct((4, width, height), jnp.bfloat16),
        cost_estimate=pl.CostEstimate(
            flops=8 * width * height * depth,
            bytes_accessed=8 * height * depth + 2 * width * depth + 8 * width * height,
            transcendentals=0,
        ),
        compiler_params=pltpu.CompilerParams(vmem_limit_bytes=12 * 1024 * 1024),
    )(factor, *blocks, *added)


def per_device(ainv, lpanel, dinv, rowblocks, counts, widths):
    prow, pcol = lax.axis_index("prow"), lax.axis_index("pcol")
    zh, y, core = prow >> 3, (prow >> 1) & 3, prow & 1
    x, zl = pcol >> 3, pcol & 7
    high, mid, low = zl >> 2, (zl >> 1) & 1, zl & 1

    own = lpanel.T
    first = send(own, lambda *d: fold_x(*d, 0))
    second = send(own, lambda *d: fold_x(*d, 1))
    pair = jnp.stack([first, second])
    near = send(pair, lambda zh, y, core, x, zl: (zh, y, core, x, zl ^ 2))
    quad = jnp.stack([pair, near], axis=1)
    last = send(quad, lambda zh, y, core, x, zl: (zh, y, core, x, zl ^ 1))

    a1 = send(ainv, lambda zh, y, core, x, zl: (zh, y, core, x ^ 1, zl))
    a3 = send(ainv, lambda zh, y, core, x, zl: (zh, y, core, x ^ 3, zl))
    half = ainv.shape[0] // 2
    a2 = [
        send(a3[:half], lambda zh, y, core, x, zl: (zh, y, core, x ^ 1, zl)),
        send(a1[half:], lambda zh, y, core, x, zl: (zh, y, core, x ^ 3, zl)),
    ]

    slots = jnp.arange(rowblocks.shape[1], dtype=jnp.int32)
    used = jnp.where(slots[None, :] < counts[:, None], rowblocks, -1)
    member = jnp.any(used[:, :, None] == jnp.arange(64, dtype=jnp.int32)[None, None, :], axis=1)
    nodes = jnp.arange(SNODES, dtype=jnp.int32)
    my_nodes = (high ^ jnp.arange(2, dtype=jnp.int32)) * 4 + x
    chosen = my_nodes[:, None] == nodes[None, :]
    my_blocks = prow * 4 + jnp.arange(4, dtype=jnp.int32)
    block_is = my_blocks[:, None] == jnp.arange(64, dtype=jnp.int32)[None, :]
    live = jnp.any(
        chosen[:, None, :, None] & block_is[None, :, None, :] & member[None, None, :, :], axis=(2, 3)
    )
    width = jnp.sum(jnp.where(chosen, widths[None, :], 0), axis=1)
    half_of = (mid ^ jnp.arange(2, dtype=jnp.int32))[:, None, None] * 128
    within = half_of + jnp.arange(128, dtype=jnp.int32).reshape(1, 2, 64)
    active = within[None] < width[:, None, None, None]

    factor = jnp.stack(
        [jnp.where(low == 0, quad, last), jnp.where(low == 0, last, quad)], axis=2
    )
    row_scale = jnp.repeat(live.astype(jnp.bfloat16), B, axis=1)
    factor = factor * active[..., None].astype(jnp.bfloat16) * row_scale[:, None, None, None, :]

    mine = lax.dynamic_slice_in_dim(factor[0, 0].reshape(128, 1024), low * 512, 512, axis=1)
    mine = send(mine, rows_home)

    keep = core ^ mid
    theirs = lax.dynamic_index_in_dim(factor, 1 - keep, 1, keepdims=False).reshape(256, 1024)
    ours = lax.dynamic_index_in_dim(factor, keep, 1, keepdims=False).reshape(256, 1024)
    ours, theirs, upper, lower = lax.optimization_barrier((ours, theirs, *a2))
    blocks = (ainv, a1, upper, lower, a3)
    away, mine = lax.optimization_barrier((partial_product(theirs, blocks), mine))
    other = send(away, lambda zh, y, core, x, zl: (zh, y, core ^ 1, x, zl))
    chip = partial_product(ours, blocks, other)

    shares = lax.all_to_all(chip, AXES, 0, 0, axis_index_groups=swap_groups())
    beside = send(mine, lambda zh, y, core, x, zl: (zh, y, core ^ 1, x, zl))
    across = jnp.concatenate([jnp.where(core == 0, mine, beside), jnp.where(core == 0, beside, mine)])
    rounded = jnp.sum(shares.astype(jnp.float32), axis=0).reshape(2, 128, 512).astype(jnp.bfloat16)

    stay = zh ^ high
    part = [lax.dynamic_index_in_dim(rounded, stay ^ k, 0, keepdims=False) for k in range(2)]
    far = send(part[1], lambda zh, y, core, x, zl: (zh ^ 1, x, core, y, zl))
    near = send(part[0], lambda zh, y, core, x, zl: (zh, x, core, y, zl))
    product = near.astype(jnp.float32) + far.astype(jnp.float32)

    terms = dot_t(across, product.astype(jnp.bfloat16)).astype(jnp.bfloat16)
    pieces = lax.all_to_all(terms.reshape(32, 8, 128), "pcol", 0, 0)
    piece = jnp.sum(pieces.astype(jnp.float32), axis=0).astype(jnp.bfloat16)
    terms = lax.all_to_all(jnp.broadcast_to(piece[None], (32, 8, 128)), "pcol", 0, 0)
    terms = terms.reshape(256, 128).astype(jnp.float32)

    node = prow >> 1
    row_ids = pcol * 2 + jnp.arange(2, dtype=jnp.int32)
    kept = jnp.any(
        (row_ids[:, None] == jnp.arange(64, dtype=jnp.int32)[None, :])[:, None, :]
        & (nodes == node)[None, :, None]
        & member[None],
        axis=(1, 2),
    )
    negated = jnp.where(kept[None, :, None], -product.reshape(128, 2, B), 0.0).reshape(128, 512)
    selected_inverse = negated.astype(jnp.bfloat16).T

    my_width = jnp.sum(jnp.where(nodes == node, widths, 0))
    column = core * 128 + jnp.arange(128, dtype=jnp.int32)
    corner = (jnp.arange(B, dtype=jnp.int32)[:, None] < my_width) & (column < my_width)[None, :]
    diagonal_blocks = jnp.where(corner, dinv, 0.0) + terms
    return (selected_inverse, diagonal_blocks)


def solution(mesh):
    placed = (P("pcol", "prow"), P("prow", "pcol"), P(None, "prow"), P(), P(), P())
    return jax.shard_map(
        per_device,
        mesh=mesh,
        in_specs=placed,
        out_specs=(P("pcol", "prow"), P(None, "prow")),
        check_vma=False,
    )
```

```python
import functools

import jax
import jax.numpy as jnp
from jax import lax
from jax.experimental import pallas as pl
from jax.experimental.pallas import tpu as pltpu
from jax.sharding import PartitionSpec as P

B = 256
SNODES = 8
AXES = ("prow", "pcol")
CONTRACT_LAST = (((1,), (1,)), ((), ()))


def send(value, target):
    pairs = []
    for source in range(512):
        row, col = source // 32, source % 32
        zh, y, core, x, zl = target(row >> 3, (row >> 1) & 3, row & 1, col >> 3, col & 7)
        pairs.append((source, ((zh * 4 + y) * 2 + core) * 32 + x * 8 + zl))
    return lax.ppermute(value, AXES, pairs)


def fold_x(zh, y, core, x, zl, flip):
    node = 2 * x + (zl >> 2)
    return (zh, y, core, node & 3, (((node >> 2) ^ flip) << 2) | (zl & 3))


def rows_home(zh, y, core, x, zl, flip):
    column = ((y & 1) << 2) | (core << 1) | ((zl & 1) ^ flip)
    return (x >> 1, ((x & 1) << 1) | (zl >> 2), (zl >> 1) & 1, (zh << 1) | (y >> 1), column)


def swap_groups():
    groups = []
    for zh in range(2):
        for core in range(2):
            for x in range(4):
                for zl in range(8):
                    groups.append(
                        [((zh * 4 + (j ^ x)) * 2 + core) * 32 + x * 8 + zl for j in range(4)]
                    )
    return groups


def dot_t(left, right):
    return lax.dot_general(left, right, CONTRACT_LAST, preferred_element_type=jnp.float32)


def product_kernel(added, factor, near, one, upper, lower, three, *rest):
    out = rest[-1]
    half = upper.shape[0]
    for place, rows in ((0, near), (1, one), (3, three)):
        term = dot_t(factor[...], rows[...])
        if added:
            term = term + rest[0][place].astype(jnp.float32)
        out[place] = term.astype(jnp.bfloat16)
    for columns, rows in ((slice(0, half), upper), (slice(half, 2 * half), lower)):
        term = dot_t(factor[...], rows[...])
        if added:
            term = term + rest[0][2, :, columns].astype(jnp.float32)
        out[2, :, columns] = term.astype(jnp.bfloat16)


def partial_product(factor, blocks, *added):
    width, depth = factor.shape
    height = blocks[0].shape[0]
    return pl.pallas_call(
        functools.partial(product_kernel, len(added)),
        in_specs=[pl.BlockSpec(memory_space=pltpu.VMEM)] * (6 + len(added)),
        out_specs=pl.BlockSpec(memory_space=pltpu.VMEM),
        out_shape=jax.ShapeDtypeStruct((4, width, height), jnp.bfloat16),
        cost_estimate=pl.CostEstimate(
            flops=8 * width * height * depth,
            bytes_accessed=8 * height * depth + 2 * width * depth + 8 * width * height,
            transcendentals=0,
        ),
        compiler_params=pltpu.CompilerParams(vmem_limit_bytes=12 * 1024 * 1024),
    )(factor, *blocks, *added)


def per_device(ainv, lpanel, dinv, rowblocks, counts, widths):
    prow, pcol = lax.axis_index("prow"), lax.axis_index("pcol")
    zh, y, core = prow >> 3, (prow >> 1) & 3, prow & 1
    x, zl = pcol >> 3, pcol & 7
    high, mid, low = zl >> 2, (zl >> 1) & 1, zl & 1

    own = lpanel.T
    first = send(own, lambda *d: fold_x(*d, 0))
    second = send(own, lambda *d: fold_x(*d, 1))
    panel, first, second = lax.optimization_barrier((own, first, second))
    pair = jnp.stack([first, second])
    mine = [
        send(
            lax.dynamic_slice_in_dim(panel, (low ^ k) * 512, 512, axis=1),
            lambda *d: rows_home(*d, k),
        )
        for k in range(2)
    ]
    near = send(pair, lambda zh, y, core, x, zl: (zh, y, core, x, zl ^ 2))
    a1 = send(ainv, lambda zh, y, core, x, zl: (zh, y, core, x ^ 1, zl))
    a3 = send(ainv, lambda zh, y, core, x, zl: (zh, y, core, x ^ 3, zl))
    quad = jnp.stack([pair, near], axis=1)
    quad, a1, a3 = lax.optimization_barrier((quad, a1, a3))
    last = send(quad, lambda zh, y, core, x, zl: (zh, y, core, x, zl ^ 1))

    half = ainv.shape[0] // 2
    a2 = [
        send(a3[:half], lambda zh, y, core, x, zl: (zh, y, core, x ^ 1, zl)),
        send(a1[half:], lambda zh, y, core, x, zl: (zh, y, core, x ^ 3, zl)),
    ]

    slots = jnp.arange(rowblocks.shape[1], dtype=jnp.int32)
    used = jnp.where(slots[None, :] < counts[:, None], rowblocks, -1)
    member = jnp.any(used[:, :, None] == jnp.arange(64, dtype=jnp.int32)[None, None, :], axis=1)
    nodes = jnp.arange(SNODES, dtype=jnp.int32)
    my_nodes = (high ^ jnp.arange(2, dtype=jnp.int32)) * 4 + x
    chosen = my_nodes[:, None] == nodes[None, :]
    my_blocks = prow * 4 + jnp.arange(4, dtype=jnp.int32)
    block_is = my_blocks[:, None] == jnp.arange(64, dtype=jnp.int32)[None, :]
    live = jnp.any(
        chosen[:, None, :, None] & block_is[None, :, None, :] & member[None, None, :, :], axis=(2, 3)
    )
    width = jnp.sum(jnp.where(chosen, widths[None, :], 0), axis=1)
    half_of = (mid ^ jnp.arange(2, dtype=jnp.int32))[:, None, None] * 128
    within = half_of + jnp.arange(128, dtype=jnp.int32).reshape(1, 2, 64)
    active = within[None] < width[:, None, None, None]

    node = prow >> 1
    row_ids = pcol * 2 + jnp.arange(2, dtype=jnp.int32)
    kept = jnp.any(
        (row_ids[:, None] == jnp.arange(64, dtype=jnp.int32)[None, :])[:, None, :]
        & (nodes == node)[None, :, None]
        & member[None],
        axis=(1, 2),
    )
    my_width = jnp.sum(jnp.where(nodes == node, widths, 0))
    column = core * 128 + jnp.arange(128, dtype=jnp.int32)
    mine = jnp.concatenate([jnp.where(low == 0, mine[0], mine[1]), jnp.where(low == 0, mine[1], mine[0])])
    mine = mine * (column < my_width).astype(jnp.bfloat16)[:, None]
    mine = mine * jnp.repeat(kept.astype(jnp.bfloat16), B)[None, :]

    factor = jnp.stack(
        [jnp.where(low == 0, quad, last), jnp.where(low == 0, last, quad)], axis=2
    )
    row_scale = jnp.repeat(live.astype(jnp.bfloat16), B, axis=1)
    factor = factor * active[..., None].astype(jnp.bfloat16) * row_scale[:, None, None, None, :]

    keep = core ^ mid
    theirs = lax.dynamic_index_in_dim(factor, 1 - keep, 1, keepdims=False).reshape(256, 1024)
    ours = lax.dynamic_index_in_dim(factor, keep, 1, keepdims=False).reshape(256, 1024)
    ours, theirs, upper, lower = lax.optimization_barrier((ours, theirs, *a2))
    blocks = (ainv, a1, upper, lower, a3)
    away, mine = lax.optimization_barrier((partial_product(theirs, blocks), mine))
    other = send(away, lambda zh, y, core, x, zl: (zh, y, core ^ 1, x, zl))
    chip = partial_product(ours, blocks, other)

    shares = lax.all_to_all(chip, AXES, 0, 0, axis_index_groups=swap_groups())
    beside = send(mine, lambda zh, y, core, x, zl: (zh, y, core ^ 1, x, zl))
    across = jnp.concatenate([jnp.where(core == 0, mine, beside), jnp.where(core == 0, beside, mine)])
    rounded = jnp.sum(shares.astype(jnp.float32), axis=0).reshape(2, 128, 512).astype(jnp.bfloat16)

    stay = zh ^ high
    part = [lax.dynamic_index_in_dim(rounded, stay ^ k, 0, keepdims=False) for k in range(2)]
    far = send(part[1], lambda zh, y, core, x, zl: (zh ^ 1, x, core, y, zl))
    near = send(part[0], lambda zh, y, core, x, zl: (zh, x, core, y, zl))
    product = near.astype(jnp.float32) + far.astype(jnp.float32)

    terms = dot_t(across, product.astype(jnp.bfloat16)).astype(jnp.bfloat16)
    pieces = lax.all_to_all(terms.reshape(32, 8, 128), "pcol", 0, 0)
    piece = jnp.sum(pieces.astype(jnp.float32), axis=0).astype(jnp.bfloat16)
    terms = lax.all_to_all(jnp.broadcast_to(piece[None], (32, 8, 128)), "pcol", 0, 0)
    terms = terms.reshape(256, 128).astype(jnp.float32)

    negated = jnp.where(kept[None, :, None], -product.reshape(128, 2, B), 0.0).reshape(128, 512)
    selected_inverse = negated.astype(jnp.bfloat16).T

    corner = (jnp.arange(B, dtype=jnp.int32)[:, None] < my_width) & (column < my_width)[None, :]
    diagonal_blocks = jnp.where(corner, dinv, 0.0) + terms
    return (selected_inverse, diagonal_blocks)


def solution(mesh):
    placed = (P("pcol", "prow"), P("prow", "pcol"), P(None, "prow"), P(), P(), P())
    return jax.shard_map(
        per_device,
        mesh=mesh,
        in_specs=placed,
        out_specs=(P("pcol", "prow"), P(None, "prow")),
        check_vma=False,
    )
```

```python
import functools

import jax
import jax.numpy as jnp
from jax import lax
from jax.experimental import pallas as pl
from jax.experimental.pallas import tpu as pltpu
from jax.sharding import PartitionSpec as P

B = 256
SNODES = 8
AXES = ("prow", "pcol")
CONTRACT_LAST = (((1,), (1,)), ((), ()))


def send(value, target):
    pairs = []
    for source in range(512):
        row, col = source // 32, source % 32
        zh, y, core, x, zl = target(row >> 3, (row >> 1) & 3, row & 1, col >> 3, col & 7)
        pairs.append((source, ((zh * 4 + y) * 2 + core) * 32 + x * 8 + zl))
    return lax.ppermute(value, AXES, pairs)


def fold_x(zh, y, core, x, zl, flip):
    node = 2 * x + (zl >> 2)
    return (zh, y, core, node & 3, (((node >> 2) ^ flip) << 2) | (zl & 3))


def rows_home(zh, y, core, x, zl, flip):
    column = ((y & 1) << 2) | (core << 1) | ((zl & 1) ^ flip)
    return (x >> 1, ((x & 1) << 1) | (zl >> 2), (zl >> 1) & 1, (zh << 1) | (y >> 1), column)


def swap_groups():
    groups = []
    for zh in range(2):
        for core in range(2):
            for x in range(4):
                for zl in range(8):
                    groups.append(
                        [((zh * 4 + (j ^ x)) * 2 + core) * 32 + x * 8 + zl for j in range(4)]
                    )
    return groups


def dot_t(left, right):
    return lax.dot_general(left, right, CONTRACT_LAST, preferred_element_type=jnp.float32)


def product_kernel(added, factor, near, one, upper, lower, three, *rest):
    out = rest[-1]
    half = upper.shape[0]
    for place, rows in ((0, near), (1, one), (3, three)):
        term = dot_t(factor[...], rows[...])
        if added:
            term = term + rest[0][place].astype(jnp.float32)
        out[place] = term.astype(jnp.bfloat16)
    for columns, rows in ((slice(0, half), upper), (slice(half, 2 * half), lower)):
        term = dot_t(factor[...], rows[...])
        if added:
            term = term + rest[0][2, :, columns].astype(jnp.float32)
        out[2, :, columns] = term.astype(jnp.bfloat16)


def partial_product(factor, blocks, *added):
    width, depth = factor.shape
    height = blocks[0].shape[0]
    return pl.pallas_call(
        functools.partial(product_kernel, len(added)),
        in_specs=[pl.BlockSpec(memory_space=pltpu.VMEM)] * (6 + len(added)),
        out_specs=pl.BlockSpec(memory_space=pltpu.VMEM),
        out_shape=jax.ShapeDtypeStruct((4, width, height), jnp.bfloat16),
        cost_estimate=pl.CostEstimate(
            flops=8 * width * height * depth,
            bytes_accessed=8 * height * depth + 2 * width * depth + 8 * width * height,
            transcendentals=0,
        ),
        compiler_params=pltpu.CompilerParams(vmem_limit_bytes=12 * 1024 * 1024),
    )(factor, *blocks, *added)


def per_device(ainv, lpanel, dinv, rowblocks, counts, widths):
    prow, pcol = lax.axis_index("prow"), lax.axis_index("pcol")
    zh, y, core = prow >> 3, (prow >> 1) & 3, prow & 1
    x, zl = pcol >> 3, pcol & 7
    high, mid, low = zl >> 2, (zl >> 1) & 1, zl & 1

    slots = jnp.arange(rowblocks.shape[1], dtype=jnp.int32)
    used = jnp.where(slots[None, :] < counts[:, None], rowblocks, -1)
    member = jnp.any(used[:, :, None] == jnp.arange(64, dtype=jnp.int32)[None, None, :], axis=1)
    nodes = jnp.arange(SNODES, dtype=jnp.int32)
    my_nodes = (high ^ jnp.arange(2, dtype=jnp.int32)) * 4 + x
    chosen = my_nodes[:, None] == nodes[None, :]
    my_blocks = prow * 4 + jnp.arange(4, dtype=jnp.int32)
    block_is = my_blocks[:, None] == jnp.arange(64, dtype=jnp.int32)[None, :]
    live = jnp.any(
        chosen[:, None, :, None] & block_is[None, :, None, :] & member[None, None, :, :], axis=(2, 3)
    )
    width = jnp.sum(jnp.where(chosen, widths[None, :], 0), axis=1)
    half_of = (mid ^ jnp.arange(2, dtype=jnp.int32))[:, None] * 128
    within = half_of + low * 64 + jnp.arange(64, dtype=jnp.int32)[None, :]
    active = (within[None] < width[:, None, None]).astype(jnp.bfloat16)
    row_scale = jnp.repeat(live.astype(jnp.bfloat16), B, axis=1)

    own = lpanel.T
    first = send(own, lambda *d: fold_x(*d, 0))
    second = send(own, lambda *d: fold_x(*d, 1))
    panel, first, second = lax.optimization_barrier((own, first, second))
    pair = jnp.stack([first, second])
    mine = [
        send(
            lax.dynamic_slice_in_dim(panel, (low ^ k) * 512, 512, axis=1),
            lambda *d: rows_home(*d, k),
        )
        for k in range(2)
    ]
    near = send(pair, lambda zh, y, core, x, zl: (zh, y, core, x, zl ^ 2))
    a1 = send(ainv, lambda zh, y, core, x, zl: (zh, y, core, x ^ 1, zl))
    a3 = send(ainv, lambda zh, y, core, x, zl: (zh, y, core, x ^ 3, zl))
    near, a1, a3 = lax.optimization_barrier((near, a1, a3))
    quad = jnp.stack([pair, near], axis=1) * active[..., None] * row_scale[:, None, None, :]
    last = send(quad, lambda zh, y, core, x, zl: (zh, y, core, x, zl ^ 1))

    half = ainv.shape[0] // 2
    a2 = [
        send(a3[:half], lambda zh, y, core, x, zl: (zh, y, core, x ^ 1, zl)),
        send(a1[half:], lambda zh, y, core, x, zl: (zh, y, core, x ^ 3, zl)),
    ]

    node = prow >> 1
    row_ids = pcol * 2 + jnp.arange(2, dtype=jnp.int32)
    kept = jnp.any(
        (row_ids[:, None] == jnp.arange(64, dtype=jnp.int32)[None, :])[:, None, :]
        & (nodes == node)[None, :, None]
        & member[None],
        axis=(1, 2),
    )
    my_width = jnp.sum(jnp.where(nodes == node, widths, 0))
    column = core * 128 + jnp.arange(128, dtype=jnp.int32)
    mine = jnp.concatenate([jnp.where(low == 0, mine[0], mine[1]), jnp.where(low == 0, mine[1], mine[0])])
    mine = mine * (column < my_width).astype(jnp.bfloat16)[:, None]
    mine = mine * jnp.repeat(kept.astype(jnp.bfloat16), B)[None, :]

    factor = jnp.stack(
        [jnp.where(low == 0, quad, last), jnp.where(low == 0, last, quad)], axis=2
    )
    keep = core ^ mid
    theirs = lax.dynamic_index_in_dim(factor, 1 - keep, 1, keepdims=False).reshape(256, 1024)
    ours = lax.dynamic_index_in_dim(factor, keep, 1, keepdims=False).reshape(256, 1024)
    ours, theirs, upper, lower = lax.optimization_barrier((ours, theirs, *a2))
    blocks = (ainv, a1, upper, lower, a3)
    away, mine = lax.optimization_barrier((partial_product(theirs, blocks), mine))
    other = send(away, lambda zh, y, core, x, zl: (zh, y, core ^ 1, x, zl))
    chip = partial_product(ours, blocks, other)

    shares = lax.all_to_all(chip, AXES, 0, 0, axis_index_groups=swap_groups())
    beside = send(mine, lambda zh, y, core, x, zl: (zh, y, core ^ 1, x, zl))
    across = jnp.concatenate([jnp.where(core == 0, mine, beside), jnp.where(core == 0, beside, mine)])
    rounded = jnp.sum(shares.astype(jnp.float32), axis=0).reshape(2, 128, 512).astype(jnp.bfloat16)

    stay = zh ^ high
    part = [lax.dynamic_index_in_dim(rounded, stay ^ k, 0, keepdims=False) for k in range(2)]
    far = send(part[1], lambda zh, y, core, x, zl: (zh ^ 1, x, core, y, zl))
    near = send(part[0], lambda zh, y, core, x, zl: (zh, x, core, y, zl))
    product = near.astype(jnp.float32) + far.astype(jnp.float32)

    terms = dot_t(across, product.astype(jnp.bfloat16)).astype(jnp.bfloat16)
    pieces = lax.all_to_all(terms.reshape(32, 8, 128), "pcol", 0, 0)
    piece = jnp.sum(pieces.astype(jnp.float32), axis=0).astype(jnp.bfloat16)
    terms = lax.all_to_all(jnp.broadcast_to(piece[None], (32, 8, 128)), "pcol", 0, 0)
    terms = terms.reshape(256, 128).astype(jnp.float32)

    negated = jnp.where(kept[None, :, None], -product.reshape(128, 2, B), 0.0).reshape(128, 512)
    selected_inverse = negated.astype(jnp.bfloat16).T

    corner = (jnp.arange(B, dtype=jnp.int32)[:, None] < my_width) & (column < my_width)[None, :]
    diagonal_blocks = jnp.where(corner, dinv, 0.0) + terms
    return (selected_inverse, diagonal_blocks)


def solution(mesh):
    placed = (P("pcol", "prow"), P("prow", "pcol"), P(None, "prow"), P(), P(), P())
    return jax.shard_map(
        per_device,
        mesh=mesh,
        in_specs=placed,
        out_specs=(P("pcol", "prow"), P(None, "prow")),
        check_vma=False,
    )
```
